512 devices in a mesh: blk: 128 (over y, x, z_lo), col: 4 (over z_hi, core).
Axes of the slice: x: 4, y: 4, z: 16 (z_hi: 2, z_lo: 8; z = z_hi * 8 + z_lo), core: 2. Of those that a mesh axis runs over, the one named last changes fastest.
Arguments:
- tile_u: bfloat16 [128, 16, 1024, 128], P('blk', 'col'), may hold values from -6 to 6
- tile_v: bfloat16 [128, 16, 1024, 128], P('blk', 'col'), may hold values from -6 to 6
- tile_rank: int32 [128, 16], P('blk', 'col'), may hold values from 32 to 128
- panel_u: bfloat16 [16, 1024, 128], P('col', 'blk'), may hold values from -6 to 6
- panel_v: bfloat16 [16, 1024, 128], P('col', 'blk'), may hold values from -0.1875 to 0.1875
- band_rank: int32 [16], P('col'), may hold values from 32 to 128
- row_u: bfloat16 [128, 1024, 128], P('blk', 'col'), may hold values from -6 to 6
- row_v: bfloat16 [128, 1024, 128], P('blk', 'col'), may hold values from -0.5 to 0.5
- row_rank: int32 [128], P('blk'), may hold values from 32 to 128
- target_rank: int32 [128, 16], P('blk', 'col'), may hold values from 32 to 128
Outputs:
- new_u: bfloat16 [128, 16, 1024, 128], P('blk', 'col')
- new_v: bfloat16 [128, 16, 1024, 128], P('blk', 'col')
The draws below stay inside these ranges and needn't reach their ends.
All inputs are finite; a program needn't handle non-finite values.
Results may differ from the reference program's by a relative error of at most 0.001.
Values may be sent and summed in bfloat16 or wider, within the bound.
No kernel may reach another device: no remote copies, remote signals or barrier semaphores. Data moves between devices by JAX's collectives and lax.ppermute only.
A program may use at most 64 MiB of HBM per device.

```python
import math
import jax
import jax.numpy as jnp
from jax import lax

NB = 1024
K = 128
BAND = 16
ROWS = 128


def with_ends(result, stream_key, smallest, largest):
    shape = result.shape
    index_at = [jax.random.randint(jax.random.fold_in(stream_key, axis), (), 0, shape[axis]) for axis in range(len(shape))]
    result = result.at[tuple(index_at)].set(smallest)
    longest = shape.index(max(shape))
    index_at[longest] = (index_at[longest] + 1) % shape[longest]
    return result.at[tuple(index_at)].set(largest)


def block_scale(rng, shape, shards, smallest, largest):
    level, own = 1.0, jax.random.fold_in(rng, 6)
    for axis_at, blocks in shards:
        steps = jnp.exp(jax.random.uniform(jax.random.fold_in(own, axis_at), (blocks,), jnp.float32, smallest / len(shards), largest / len(shards)))
        level = level * jnp.repeat(steps, shape[axis_at] // blocks).reshape([-1 if axis == axis_at else 1 for axis in range(len(shape))])
    return level


def gaussian(own_key, shape, width, limit, split=(), kind=jnp.bfloat16):
    drawn = width * jax.random.normal(own_key, shape, jnp.float32)
    if split:
        drawn = drawn * block_scale(own_key, shape, split, -0.22, 0.18)
    return jnp.clip(drawn, -limit, limit).astype(kind)


def setup_inputs(seed: int = 0) -> dict:
    streams_of = jax.random.split(jax.random.key(seed), 11)
    tile_u = gaussian(streams_of[0], (ROWS, BAND, NB, K), 1.0, 6.0, ((0, 128), (1, 4)))
    tile_v = gaussian(streams_of[1], (ROWS, BAND, NB, K), 1.0, 6.0, ((0, 128), (1, 4)))
    tile_rank = with_ends(jax.random.randint(streams_of[2], (ROWS, BAND), K // 4, K + 1), jax.random.fold_in(streams_of[2], 1), K // 4, K).astype(jnp.int32)
    panel_u = gaussian(streams_of[3], (BAND, NB, K), 1.0, 6.0, ((0, 4), (1, 128)))
    panel_v = gaussian(streams_of[4], (BAND, NB, K), NB ** -0.5, 0.1875, ((0, 4), (1, 128)))
    band_rank = with_ends(jax.random.randint(streams_of[5], (BAND,), K // 4, K + 1), jax.random.fold_in(streams_of[5], 1), K // 4, K).astype(jnp.int32)
    row_u = gaussian(streams_of[6], (ROWS, NB, K), 1.0, 6.0, ((0, 128), (1, 4)))
    row_v = gaussian(streams_of[7], (ROWS, NB, K), K ** -0.5, 0.5, ((0, 128), (1, 4)))
    row_rank = with_ends(jax.random.randint(streams_of[8], (ROWS,), K // 4, K + 1), jax.random.fold_in(streams_of[8], 1), K // 4, K).astype(jnp.int32)
    target_rank = with_ends(jax.random.randint(streams_of[9], (ROWS, BAND), K // 4, K + 1), jax.random.fold_in(streams_of[9], 1), K // 4, K).astype(jnp.int32)
    return dict(tile_u=tile_u, tile_v=tile_v, tile_rank=tile_rank, panel_u=panel_u, panel_v=panel_v, band_rank=band_rank, row_u=row_u, row_v=row_v, row_rank=row_rank, target_rank=target_rank)


HIGH = lax.Precision.HIGHEST

def pair_columns(first, second):
    joined = jnp.stack([first, second], axis=-1)
    return joined.reshape(joined.shape[:-2] + (joined.shape[-2] * 2,))

def one_row(items, panel_u, panel_v, band_rank):
    tile_u, tile_v, tile_rank, row_u, row_v, row_rank, target_rank = items
    lane = jnp.arange(K)
    row_keep = (lane < row_rank).astype(jnp.bfloat16)
    tile_keep = (lane[None, :] < tile_rank[:, None]).astype(jnp.bfloat16)
    band_keep = (lane[None, :] < band_rank[:, None]).astype(jnp.bfloat16)
    left_row = row_u * row_keep[None, :]
    right_row = (row_v * row_keep[None, :]).astype(jnp.float32)
    left_tile = tile_u * tile_keep[:, None, :]
    right_tile = (tile_v * tile_keep[:, None, :]).astype(jnp.float32)
    pu_masked = (panel_u * band_keep[:, None, :]).astype(jnp.float32)
    pv_masked = (panel_v * band_keep[:, None, :]).astype(jnp.float32)
    core = jnp.einsum('nk,jnl->jkl', right_row, pv_masked, precision=HIGH)
    right_panel = -jnp.einsum('jnl,jkl->jnk', pu_masked, core, precision=HIGH)
    left = pair_columns(left_tile, jnp.broadcast_to(left_row, left_tile.shape))
    right = pair_columns(right_tile, right_panel)
    spare = 1.0 - pair_columns(tile_keep.astype(jnp.float32), jnp.broadcast_to(row_keep.astype(jnp.float32), tile_keep.shape))
    gram = jnp.einsum('jnk,jnl->jkl', left.astype(jnp.float32), left.astype(jnp.float32), preferred_element_type=jnp.float32)
    gram = gram + spare[:, :, None] * jnp.eye(2 * K, dtype=jnp.float32)[None]
    lower = jnp.linalg.cholesky(gram)
    ortho = lax.linalg.triangular_solve(lower, left.astype(jnp.float32), left_side=False, lower=True, transpose_a=True)
    target_keep = (lane[None, :] < target_rank[:, None]).astype(jnp.float32)
    scale = math.sqrt(NB)
    new_u = ortho[:, :, :K] * scale * target_keep[:, None, :]
    head = jnp.transpose(lower, (0, 2, 1))[:, :K, :]
    new_v = jnp.einsum('jnc,jmc->jnm', right, head, precision=HIGH) / scale
    new_v = new_v * target_keep[:, None, :]
    return (new_u.astype(jnp.bfloat16), new_v.astype(jnp.bfloat16))

def reference(tile_u, tile_v, tile_rank, panel_u, panel_v, band_rank, row_u, row_v, row_rank, target_rank):

    def step(items):
        return one_row(items, panel_u, panel_v, band_rank)
    return lax.map(step, (tile_u, tile_v, tile_rank, row_u, row_v, row_rank, target_rank))
```

```python
import math

import jax
import jax.numpy as jnp
from jax import lax
from jax.experimental import pallas as pl
from jax.experimental.pallas import tpu as pltpu
from jax.sharding import Mesh, PartitionSpec as P

F32, BF16 = jnp.float32, jnp.bfloat16
HIGH = lax.Precision.HIGHEST
STEP = 8


def dot(a, b, dims, precision=None):
    return lax.dot_general(
        a, b, (dims, ((), ())), precision=precision, preferred_element_type=F32
    )


def three_parts(x):
    high = x.astype(BF16).astype(F32)
    rest = x - high
    middle = rest.astype(BF16).astype(F32)
    return high, middle, rest - middle


def spread(row):
    return jnp.broadcast_to(row, (STEP, row.shape[1]))


def factor_panel(panel, inverse, first):
    width = panel.shape[1]
    sub = lax.broadcasted_iota(jnp.int32, (STEP, width), 0)
    column = [
        jnp.broadcast_to(panel[:, first + s : first + s + 1], (STEP, width)) for s in range(STEP)
    ]
    for s in range(STEP - 1):
        ratio = jnp.where(sub > s, column[s] / spread(column[s][s : s + 1]), 0.0)
        panel = panel - ratio * spread(panel[s : s + 1])
        inverse = inverse - ratio * spread(inverse[s : s + 1])
        for u in range(s + 1, STEP):
            column[u] = column[u] - ratio * spread(column[u][s : s + 1])
    pivot = column[0]
    for s in range(1, STEP):
        pivot = jnp.where(sub == s, column[s], pivot)
    scale = lax.rsqrt(pivot)
    scale = scale * (1.5 - 0.5 * pivot * scale * scale)
    return panel * scale, inverse * scale


def left_kernel(
    tile_rank, row_rank, target_rank, place, tile_u, near, far, new_u, head, gram, lower_inv
):
    tiles, order, width = tile_u.shape
    quarter = order // 4
    lane = lax.broadcasted_iota(jnp.int32, (width, width), 1)
    sub = lax.broadcasted_iota(jnp.int32, (width, width), 0)
    rows = []
    for q in range(4):
        mine, other = place[0] ^ (q // 2), place[1] ^ (q % 2)
        rows.append(jnp.where(other == 0, near[mine, 0], far[mine, 0]))
    left_row = jnp.concatenate(rows, axis=0)
    pick_row = jnp.where((lane == 2 * sub + 1) & (sub < row_rank[0]), 1.0, 0.0)
    firsts, sides = [], []
    for t in range(tiles):
        pick_tile = jnp.where((lane == 2 * sub) & (sub < tile_rank[0, t]), 1.0, 0.0)
        pick = jnp.concatenate([pick_tile, pick_row], axis=0).astype(BF16)
        both = jnp.concatenate([tile_u[t], left_row], axis=1)
        first = dot(both, pick, ((1,), (0,))).astype(BF16)
        side = dot(first, jnp.concatenate([both, first], axis=1), ((0,), (0,)))
        half = sub // 2
        rank = jnp.where(sub % 2 == 0, tile_rank[0, t], row_rank[0])
        unit = jnp.where(lane == sub, 1.0, 0.0)
        gram[t, :, :width] = side[:, 2 * width :] + jnp.where(half >= rank, unit, 0.0)
        gram[t, :, width:] = unit
        firsts.append(first)
        tile_side = jnp.where(lane < tile_rank[0, t], side[:, :width], 0.0)
        row_side = jnp.where(lane < row_rank[0], side[:, width : 2 * width], 0.0)
        sides.append(jnp.concatenate([tile_side, row_side], axis=1))
    for first in range(0, width, STEP):
        later = first + STEP
        for t in range(tiles):
            upper, inverse = factor_panel(
                gram[t, first:later, :width], gram[t, first:later, width:], first
            )
            lower_inv[t, first:later, :] = inverse
            if later < width:
                uh, um, ul = three_parts(upper)
                ih, im, il = three_parts(inverse)
                a = jnp.concatenate([uh, uh, um, uh, um, ul], axis=0).astype(BF16)
                b = jnp.concatenate(
                    [
                        jnp.concatenate([uh, um, uh, ul, um, uh], axis=0),
                        jnp.concatenate([ih, im, ih, il, im, ih], axis=0),
                    ],
                    axis=1,
                ).astype(BF16)
                change = dot(a, b, ((0,), (0,)))
                gram[t, later:, :] = gram[t, later:, :] - change[later:, :]
    scale = math.sqrt(order)
    for t in range(tiles):
        solved = jnp.where(sub < target_rank[0, t], lower_inv[t], 0.0)
        head[t] = dot(solved, sides[t], ((1,), (0,)), HIGH) / scale
        solved = solved * scale
        high = solved.astype(BF16)
        low = (solved - high.astype(F32)).astype(BF16)
        new_u[0, t] = dot(
            jnp.concatenate([firsts[t], firsts[t]], axis=1),
            jnp.concatenate([high, low], axis=1),
            ((1,), (1,)),
        ).astype(BF16)


def right_kernel(band_rank, place, tile_v, near, far, panels, head, new_v):
    tiles, order, width = tile_v.shape
    rows = []
    for q in range(4):
        mine, other = place[0] ^ (q // 2), place[1] ^ (q % 2)
        rows.append(jnp.where(other == 0, near[mine, 1], far[mine, 1]))
    right_row = jnp.concatenate(rows, axis=0)
    lane = lax.broadcasted_iota(jnp.int32, (width, width), 1)

    def panel(which):
        found = []
        for pair in range(0, tiles, 2):
            at = (which * tiles + pair) * STEP
            wide = panels[:, at : at + 2 * STEP, :].astype(F32)
            found.append(wide[:, :STEP].reshape(order, width).astype(BF16))
            found.append(wide[:, STEP:].reshape(order, width).astype(BF16))
        return found

    panel_u, panel_v = panel(0), panel(1)
    core = dot(right_row, jnp.concatenate(panel_v, axis=1), ((0,), (0,)))
    for t in range(tiles):
        mixed = dot(head[t, :, width:], core[:, t * width : (t + 1) * width], ((1,), (0,)), HIGH)
        mixed = jnp.where(lane < band_rank[t], -mixed, 0.0)
        weight = jnp.concatenate([head[t, :, :width], mixed], axis=1)
        high = weight.astype(BF16)
        low = (weight - high.astype(F32)).astype(BF16)
        both = jnp.concatenate([tile_v[t], panel_u[t]], axis=1)
        value = dot(both, jnp.concatenate([high, low], axis=0), ((1,), (1,)))
        new_v[0, t] = (value[:, :width] + value[:, width:]).astype(BF16)


SMEM = pl.BlockSpec(memory_space=pltpu.SMEM)
VMEM = pl.BlockSpec(memory_space=pltpu.VMEM)
LIMIT = 40 * 1024 * 1024


def left_side(tile_rank, row_rank, target_rank, place, tile_u, near, far):
    tiles, order, width = tile_u.shape
    return pl.pallas_call(
        left_kernel,
        out_shape=(
            jax.ShapeDtypeStruct((1, tiles, order, width), BF16),
            jax.ShapeDtypeStruct((tiles, width, 2 * width), F32),
        ),
        in_specs=[SMEM] * 4 + [VMEM] * 3,
        out_specs=(VMEM, VMEM),
        scratch_shapes=[
            pltpu.VMEM((tiles, width, 2 * width), F32),
            pltpu.VMEM((tiles, width, width), F32),
        ],
        compiler_params=pltpu.CompilerParams(vmem_limit_bytes=LIMIT),
        cost_estimate=pl.CostEstimate(
            flops=int(1e10), bytes_accessed=int(40e6), transcendentals=0
        ),
        name="left_side",
    )(tile_rank, row_rank, target_rank, place, tile_u, near, far)


def right_side(band_rank, place, tile_v, near, far, panels, head):
    tiles, order, width = tile_v.shape
    return pl.pallas_call(
        right_kernel,
        out_shape=jax.ShapeDtypeStruct((1, tiles, order, width), BF16),
        in_specs=[SMEM] * 2 + [VMEM] * 5,
        out_specs=VMEM,
        compiler_params=pltpu.CompilerParams(vmem_limit_bytes=LIMIT),
        cost_estimate=pl.CostEstimate(
            flops=int(2e9), bytes_accessed=int(10e6), transcendentals=0
        ),
        name="right_side",
    )(band_rank, place, tile_v, near, far, panels, head)


def from_all(x, axes, size):
    copies = jnp.broadcast_to(x[None], (size,) + x.shape)
    return lax.all_to_all(copies, axes, 0, 0, tiled=True)


def swap(x, axis):
    return lax.ppermute(x, axis, [(0, 1), (1, 0)])


def on_device(
    tile_u, tile_v, tile_rank, panel_u, panel_v, band_rank, row_u, row_v, row_rank, target_rank
):
    tiles, share, width = panel_u.shape
    row = jnp.concatenate([row_u, row_v], axis=0)
    panel = jnp.concatenate([panel_u, panel_v], axis=0).reshape(2 * tiles * share, width)
    across = swap(row, "zh")
    line = from_all(panel, "z", 8)
    panels = from_all(line, ("y", "x"), 16)
    near = jnp.stack([row, across])
    far = swap(near, "core")
    place = jnp.stack([lax.axis_index("zh"), lax.axis_index("core")]).astype(jnp.int32)
    new_u, head = left_side(tile_rank, row_rank, target_rank, place, tile_u[0], near, far)
    panels = panels.reshape(128, 2 * tiles * share, width)
    new_v = right_side(band_rank, place, tile_v[0], near, far, panels, head)
    return new_u, new_v


def solution(mesh):
    fine = Mesh(mesh.devices.reshape(4, 4, 8, 2, 2), ("y", "x", "z", "zh", "core"))
    blk, col = ("y", "x", "z"), ("zh", "core")
    return jax.shard_map(
        on_device,
        mesh=fine,
        in_specs=(
            P(blk, col, None, None),
            P(blk, col, None, None),
            P(blk, col),
            P(col, blk, None),
            P(col, blk, None),
            P(col),
            P(blk, col, None),
            P(blk, col, None),
            P(blk),
            P(blk, col),
        ),
        out_specs=(P(blk, col, None, None), P(blk, col, None, None)),
        check_vma=False,
    )
```

```python
import math

import jax
import jax.numpy as jnp
from jax import lax
from jax.experimental import pallas as pl
from jax.experimental.pallas import tpu as pltpu
from jax.sharding import Mesh, PartitionSpec as P

F32, BF16 = jnp.float32, jnp.bfloat16
HIGH = lax.Precision.HIGHEST
STEP = 8


def dot(a, b, dims, precision=None):
    return lax.dot_general(
        a, b, (dims, ((), ())), precision=precision, preferred_element_type=F32
    )


def three_parts(x):
    high = x.astype(BF16).astype(F32)
    rest = x - high
    middle = rest.astype(BF16).astype(F32)
    return high, middle, rest - middle


def spread(row):
    return jnp.broadcast_to(row, (STEP, row.shape[1]))


def factor_panel(panel, inverse, first):
    width = panel.shape[1]
    sub = lax.broadcasted_iota(jnp.int32, (STEP, width), 0)
    column = [
        jnp.broadcast_to(panel[:, first + s : first + s + 1], (STEP, width)) for s in range(STEP)
    ]
    for s in range(STEP - 1):
        ratio = jnp.where(sub > s, column[s] / spread(column[s][s : s + 1]), 0.0)
        panel = panel - ratio * spread(panel[s : s + 1])
        inverse = inverse - ratio * spread(inverse[s : s + 1])
        for u in range(s + 1, STEP):
            column[u] = column[u] - ratio * spread(column[u][s : s + 1])
    pivot = column[0]
    for s in range(1, STEP):
        pivot = jnp.where(sub == s, column[s], pivot)
    scale = lax.rsqrt(pivot)
    scale = scale * (1.5 - 0.5 * pivot * scale * scale)
    return panel * scale, inverse * scale


def left_kernel(
    tile_rank, row_rank, target_rank, place, tile_u, near, far, new_u, head, gram, lower_inv
):
    tiles, order, width = tile_u.shape
    quarter = order // 4
    lane = lax.broadcasted_iota(jnp.int32, (width, width), 1)
    sub = lax.broadcasted_iota(jnp.int32, (width, width), 0)
    rows = []
    for q in range(4):
        mine, other = place[0] ^ (q // 2), place[1] ^ (q % 2)
        rows.append(jnp.where(other == 0, near[mine, 0], far[mine, 0]))
    left_row = jnp.concatenate(rows, axis=0)
    pick_row = jnp.where((lane == 2 * sub + 1) & (sub < row_rank[0]), 1.0, 0.0)
    firsts, sides = [], []
    for t in range(tiles):
        pick_tile = jnp.where((lane == 2 * sub) & (sub < tile_rank[0, t]), 1.0, 0.0)
        pick = jnp.concatenate([pick_tile, pick_row], axis=0).astype(BF16)
        both = jnp.concatenate([tile_u[t], left_row], axis=1)
        first = dot(both, pick, ((1,), (0,))).astype(BF16)
        side = dot(first, jnp.concatenate([both, first], axis=1), ((0,), (0,)))
        half = sub // 2
        rank = jnp.where(sub % 2 == 0, tile_rank[0, t], row_rank[0])
        unit = jnp.where(lane == sub, 1.0, 0.0)
        gram[t, :, :width] = side[:, 2 * width :] + jnp.where(half >= rank, unit, 0.0)
        gram[t, :, width:] = unit
        firsts.append(first)
        tile_side = jnp.where(lane < tile_rank[0, t], side[:, :width], 0.0)
        row_side = jnp.where(lane < row_rank[0], side[:, width : 2 * width], 0.0)
        sides.append(jnp.concatenate([tile_side, row_side], axis=1))
    for first in range(0, width, STEP):
        later = first + STEP
        for t in range(tiles):
            upper, inverse = factor_panel(
                gram[t, first:later, :width], gram[t, first:later, width:], first
            )
            lower_inv[t, first:later, :] = inverse
            if later < width:
                uh, um, ul = three_parts(upper)
                ih, im, il = three_parts(inverse)
                a = jnp.concatenate([uh, uh, um, uh, um, ul], axis=0).astype(BF16)
                b = jnp.concatenate(
                    [
                        jnp.concatenate([uh, um, uh, ul, um, uh], axis=0),
                        jnp.concatenate([ih, im, ih, il, im, ih], axis=0),
                    ],
                    axis=1,
                ).astype(BF16)
                change = dot(a, b, ((0,), (0,)))
                gram[t, later:, :] = gram[t, later:, :] - change[later:, :]
    scale = math.sqrt(order)
    for t in range(tiles):
        solved = jnp.where(sub < target_rank[0, t], lower_inv[t], 0.0)
        head[t] = dot(solved, sides[t], ((1,), (0,)), HIGH) / scale
        solved = solved * scale
        high = solved.astype(BF16)
        low = (solved - high.astype(F32)).astype(BF16)
        new_u[0, t] = dot(
            jnp.concatenate([firsts[t], firsts[t]], axis=1),
            jnp.concatenate([high, low], axis=1),
            ((1,), (1,)),
        ).astype(BF16)


def right_kernel(band_rank, place, tile_v, near, far, panels, head, new_v, out_at, sems):
    tiles, order, width = tile_v.shape
    rows = []
    for q in range(4):
        mine, other = place[0] ^ (q // 2), place[1] ^ (q % 2)
        rows.append(jnp.where(other == 0, near[mine, 1], far[mine, 1]))
    right_row = jnp.concatenate(rows, axis=0)
    lane = lax.broadcasted_iota(jnp.int32, (width, width), 1)

    def panel(which):
        found = []
        for pair in range(0, tiles, 2):
            at = (which * tiles + pair) * STEP
            wide = panels[:, at : at + 2 * STEP, :].astype(F32)
            found.append(wide[:, :STEP].reshape(order, width).astype(BF16))
            found.append(wide[:, STEP:].reshape(order, width).astype(BF16))
        return found

    core = dot(right_row, jnp.concatenate(panel(1), axis=1), ((0,), (0,)))
    panel_u = panel(0)
    stores = []
    for t in range(tiles):
        mixed = dot(head[t, :, width:], core[:, t * width : (t + 1) * width], ((1,), (0,)), HIGH)
        mixed = jnp.where(lane < band_rank[t], -mixed, 0.0)
        weight = jnp.concatenate([head[t, :, :width], mixed], axis=1)
        high = weight.astype(BF16)
        low = (weight - high.astype(F32)).astype(BF16)
        both = jnp.concatenate([tile_v[t], panel_u[t]], axis=1)
        value = dot(both, jnp.concatenate([high, low], axis=0), ((1,), (1,)))
        out_at[t] = (value[:, :width] + value[:, width:]).astype(BF16)
        stores.append(pltpu.make_async_copy(out_at.at[t], new_v.at[0, t], sems.at[t]))
        stores[t].start()
    for store in stores:
        store.wait()


SMEM = pl.BlockSpec(memory_space=pltpu.SMEM)
VMEM = pl.BlockSpec(memory_space=pltpu.VMEM)
ANY = pl.BlockSpec(memory_space=pl.ANY)
LIMIT = 16 * 1024 * 1024


def left_side(tile_rank, row_rank, target_rank, place, tile_u, near, far):
    tiles, order, width = tile_u.shape
    return pl.pallas_call(
        left_kernel,
        out_shape=(
            jax.ShapeDtypeStruct((1, tiles, order, width), BF16),
            jax.ShapeDtypeStruct((tiles, width, 2 * width), F32),
        ),
        in_specs=[SMEM] * 4 + [VMEM] * 3,
        out_specs=(VMEM, VMEM),
        scratch_shapes=[
            pltpu.VMEM((tiles, width, 2 * width), F32),
            pltpu.VMEM((tiles, width, width), F32),
        ],
        compiler_params=pltpu.CompilerParams(vmem_limit_bytes=LIMIT),
        cost_estimate=pl.CostEstimate(
            flops=int(17e9), bytes_accessed=int(40e6), transcendentals=int(1e12)
        ),
        name="left_side",
    )(tile_rank, row_rank, target_rank, place, tile_u, near, far)


def right_side(band_rank, place, tile_v, near, far, panels, head):
    tiles, order, width = tile_v.shape
    return pl.pallas_call(
        right_kernel,
        out_shape=jax.ShapeDtypeStruct((1, tiles, order, width), BF16),
        in_specs=[SMEM] * 2 + [VMEM] * 5,
        out_specs=ANY,
        scratch_shapes=[
            pltpu.VMEM((tiles, order, width), BF16),
            pltpu.SemaphoreType.DMA((tiles,)),
        ],
        compiler_params=pltpu.CompilerParams(vmem_limit_bytes=LIMIT),
        cost_estimate=pl.CostEstimate(
            flops=int(2e9), bytes_accessed=int(10e6), transcendentals=0
        ),
        name="right_side",
    )(band_rank, place, tile_v, near, far, panels, head)


def copies_kernel(line, out):
    for k in range(out.shape[0]):
        out[k] = line[...]


def copies_of(line, size):
    return pl.pallas_call(
        copies_kernel,
        out_shape=jax.ShapeDtypeStruct((size,) + line.shape, line.dtype),
        in_specs=[VMEM],
        out_specs=VMEM,
        compiler_params=pltpu.CompilerParams(vmem_limit_bytes=LIMIT),
        name="copies",
    )(line)


def prepare_kernel(panel_u, panel_v, row_u, row_v, line, row, share, sems):
    sources = (panel_u, panel_v, row_u.at[0], row_v.at[0])
    targets = (share.at[0], share.at[1], row.at[0, 0], row.at[0, 1])
    copies = [
        pltpu.make_async_copy(sources[k], targets[k], sems.at[k]) for k in range(len(sources))
    ]
    for copy in copies:
        copy.start()
    copies[0].wait()
    copies[1].wait()
    both = share[...].astype(F32).reshape(line.shape[1:]).astype(BF16)
    line[...] = jnp.broadcast_to(both[None], line.shape)
    copies[2].wait()
    copies[3].wait()


def prepare(panel_u, panel_v, row_u, row_v, size):
    tiles, share, width = panel_u.shape
    return pl.pallas_call(
        prepare_kernel,
        out_shape=(
            jax.ShapeDtypeStruct((size, 2 * tiles * share, width), BF16),
            jax.ShapeDtypeStruct((1, 2) + row_u.shape[1:], BF16),
        ),
        in_specs=[ANY] * 4,
        out_specs=(VMEM, VMEM),
        scratch_shapes=[
            pltpu.VMEM((2,) + panel_u.shape, BF16),
            pltpu.SemaphoreType.DMA((4,)),
        ],
        compiler_params=pltpu.CompilerParams(vmem_limit_bytes=None),
        cost_estimate=pl.CostEstimate(
            flops=int(1e8), bytes_accessed=int(1e6), transcendentals=0
        ),
        name="prepare",
    )(panel_u, panel_v, row_u, row_v)


def join_kernel(row, across, near):
    near[0] = row[0]
    near[1] = across[0]


def join(row, across):
    return pl.pallas_call(
        join_kernel,
        out_shape=jax.ShapeDtypeStruct((2,) + row.shape[1:], row.dtype),
        in_specs=[VMEM] * 2,
        out_specs=VMEM,
        compiler_params=pltpu.CompilerParams(vmem_limit_bytes=LIMIT),
        name="join",
    )(row, across)


def swap(x, axis):
    return lax.ppermute(x, axis, [(0, 1), (1, 0)])


def on_device(
    tile_u, tile_v, tile_rank, panel_u, panel_v, band_rank, row_u, row_v, row_rank, target_rank
):
    tiles, share, width = panel_u.shape
    copies, row = prepare(panel_u, panel_v, row_u, row_v, 8)
    across = swap(row, "zh")
    line = lax.all_to_all(copies, "z", 0, 0, tiled=True)
    copies = copies_of(line, 16)
    panels = lax.all_to_all(copies, ("y", "x"), 0, 0, tiled=True)
    near = join(row, across)
    panels = lax.all_to_all(copies, ("y", "x"), 0, 0, tiled=True)
    far = swap(near, "core")
    place = jnp.stack([lax.axis_index("zh"), lax.axis_index("core")]).astype(jnp.int32)
    new_u, head = left_side(tile_rank, row_rank, target_rank, place, tile_u[0], near, far)
    panels = panels.reshape(128, 2 * tiles * share, width)
    new_v = right_side(band_rank, place, tile_v[0], near, far, panels, head)
    return new_u, new_v


def solution(mesh):
    fine = Mesh(mesh.devices.reshape(4, 4, 8, 2, 2), ("y", "x", "z", "zh", "core"))
    blk, col = ("y", "x", "z"), ("zh", "core")
    return jax.shard_map(
        on_device,
        mesh=fine,
        in_specs=(
            P(blk, col, None, None),
            P(blk, col, None, None),
            P(blk, col),
            P(col, blk, None),
            P(col, blk, None),
            P(col),
            P(blk, col, None),
            P(blk, col, None),
            P(blk),
            P(blk, col),
        ),
        out_specs=(P(blk, col, None, None), P(blk, col, None, None)),
        check_vma=False,
    )
```

```python
import math

import jax
import jax.numpy as jnp
from jax import lax
from jax.experimental import pallas as pl
from jax.experimental.pallas import tpu as pltpu
from jax.sharding import Mesh, PartitionSpec as P

F32, BF16 = jnp.float32, jnp.bfloat16
HIGH = lax.Precision.HIGHEST
STEP = 8
ORDER = [3, 4, 2, 5, 1, 6, 0, 7]


def dot(a, b, dims, precision=None):
    return lax.dot_general(
        a, b, (dims, ((), ())), precision=precision, preferred_element_type=F32
    )


def three_parts(x):
    high = x.astype(BF16).astype(F32)
    rest = x - high
    middle = rest.astype(BF16).astype(F32)
    return high, middle, rest - middle


def spread(row):
    return jnp.broadcast_to(row, (STEP, row.shape[1]))


def factor_panel(panel, inverse, first):
    width = panel.shape[1]
    sub = lax.broadcasted_iota(jnp.int32, (STEP, width), 0)
    column = [
        jnp.broadcast_to(panel[:, first + s : first + s + 1], (STEP, width)) for s in range(STEP)
    ]
    for s in range(STEP - 1):
        ratio = jnp.where(sub > s, column[s] / spread(column[s][s : s + 1]), 0.0)
        panel = panel - ratio * spread(panel[s : s + 1])
        inverse = inverse - ratio * spread(inverse[s : s + 1])
        for u in range(s + 1, STEP):
            column[u] = column[u] - ratio * spread(column[u][s : s + 1])
    pivot = column[0]
    for s in range(1, STEP):
        pivot = jnp.where(sub == s, column[s], pivot)
    scale = lax.rsqrt(pivot)
    scale = scale * (1.5 - 0.5 * pivot * scale * scale)
    return panel * scale, inverse * scale


def left_kernel(
    tile_rank, row_rank, target_rank, place, tile_u, near, far, new_u, head, gram, lower_inv
):
    tiles, order, width = tile_u.shape
    quarter = order // 4
    lane = lax.broadcasted_iota(jnp.int32, (width, width), 1)
    sub = lax.broadcasted_iota(jnp.int32, (width, width), 0)
    rows = []
    for q in range(4):
        mine, other = place[0] ^ (q // 2), place[1] ^ (q % 2)
        rows.append(jnp.where(other == 0, near[mine, 0], far[mine, 0]))
    left_row = jnp.concatenate(rows, axis=0)
    pick_row = jnp.where((lane == 2 * sub + 1) & (sub < row_rank[0]), 1.0, 0.0)
    firsts, sides = [], []
    for t in range(tiles):
        pick_tile = jnp.where((lane == 2 * sub) & (sub < tile_rank[0, t]), 1.0, 0.0)
        pick = jnp.concatenate([pick_tile, pick_row], axis=0).astype(BF16)
        both = jnp.concatenate([tile_u[t], left_row], axis=1)
        first = dot(both, pick, ((1,), (0,))).astype(BF16)
        side = dot(first, jnp.concatenate([both, first], axis=1), ((0,), (0,)))
        half = sub // 2
        rank = jnp.where(sub % 2 == 0, tile_rank[0, t], row_rank[0])
        unit = jnp.where(lane == sub, 1.0, 0.0)
        gram[t, :, :width] = side[:, 2 * width :] + jnp.where(half >= rank, unit, 0.0)
        gram[t, :, width:] = unit
        firsts.append(first)
        tile_side = jnp.where(lane < tile_rank[0, t], side[:, :width], 0.0)
        row_side = jnp.where(lane < row_rank[0], side[:, width : 2 * width], 0.0)
        sides.append(jnp.concatenate([tile_side, row_side], axis=1))
    for first in range(0, width, STEP):
        later = first + STEP
        for t in range(tiles):
            upper, inverse = factor_panel(
                gram[t, first:later, :width], gram[t, first:later, width:], first
            )
            lower_inv[t, first:later, :] = inverse
            if later < width:
                uh, um, ul = three_parts(upper)
                ih, im, il = three_parts(inverse)
                a = jnp.concatenate([uh, uh, um, uh, um, ul], axis=0).astype(BF16)
                b = jnp.concatenate(
                    [
                        jnp.concatenate([uh, um, uh, ul, um, uh], axis=0),
                        jnp.concatenate([ih, im, ih, il, im, ih], axis=0),
                    ],
                    axis=1,
                ).astype(BF16)
                change = dot(a, b, ((0,), (0,)))
                gram[t, later:, :] = gram[t, later:, :] - change[later:, :]
    scale = math.sqrt(order)
    for t in range(tiles):
        solved = jnp.where(sub < target_rank[0, t], lower_inv[t], 0.0)
        head[t] = dot(solved, sides[t], ((1,), (0,)), HIGH) / scale
        solved = solved * scale
        high = solved.astype(BF16)
        low = (solved - high.astype(F32)).astype(BF16)
        new_u[0, t] = dot(
            jnp.concatenate([firsts[t], firsts[t]], axis=1),
            jnp.concatenate([high, low], axis=1),
            ((1,), (1,)),
        ).astype(BF16)


def right_kernel(band_rank, place, tile_v, near, far, panels, head, new_v, out_at, sems):
    tiles, order, width = tile_v.shape
    rows = []
    for q in range(4):
        mine, other = place[0] ^ (q // 2), place[1] ^ (q % 2)
        rows.append(jnp.where(other == 0, near[mine, 1], far[mine, 1]))
    right_row = jnp.concatenate(rows, axis=0)
    lane = lax.broadcasted_iota(jnp.int32, (width, width), 1)

    def panel_pair(which, pair):
        at = (which * tiles + pair) * STEP
        wide = panels[:, at : at + 2 * STEP, :].astype(F32)
        wide = wide.reshape(-1, len(ORDER), 2 * STEP, width)
        wide = jnp.stack([wide[:, ORDER.index(z)] for z in range(len(ORDER))], axis=1)
        return [
            wide[:, :, :STEP].reshape(order, width).astype(BF16),
            wide[:, :, STEP:].reshape(order, width).astype(BF16),
        ]

    panel_v = panel_pair(1, 0) + panel_pair(1, 2)
    core = dot(right_row, jnp.concatenate(panel_v, axis=1), ((0,), (0,)))
    weights = []
    for t in range(tiles):
        mixed = dot(head[t, :, width:], core[:, t * width : (t + 1) * width], ((1,), (0,)), HIGH)
        mixed = jnp.where(lane < band_rank[t], -mixed, 0.0)
        weight = jnp.concatenate([head[t, :, :width], mixed], axis=1)
        high = weight.astype(BF16)
        low = (weight - high.astype(F32)).astype(BF16)
        weights.append((high, low))
    stores = []
    for t in range(tiles):
        if t % 2 == 0:
            panel_u = panel_pair(0, t)
        high, low = weights[t]
        both = jnp.concatenate([tile_v[t], panel_u[t % 2]], axis=1)
        value = dot(both, jnp.concatenate([high, low], axis=0), ((1,), (1,)))
        out_at[t] = (value[:, :width] + value[:, width:]).astype(BF16)
        stores.append(pltpu.make_async_copy(out_at.at[t], new_v.at[0, t], sems.at[t]))
        stores[t].start()
    for store in stores:
        store.wait()


SMEM = pl.BlockSpec(memory_space=pltpu.SMEM)
VMEM = pl.BlockSpec(memory_space=pltpu.VMEM)
ANY = pl.BlockSpec(memory_space=pl.ANY)
LIMIT = 16 * 1024 * 1024


def left_side(tile_rank, row_rank, target_rank, place, tile_u, near, far):
    tiles, order, width = tile_u.shape
    return pl.pallas_call(
        left_kernel,
        out_shape=(
            jax.ShapeDtypeStruct((1, tiles, order, width), BF16),
            jax.ShapeDtypeStruct((tiles, width, 2 * width), F32),
        ),
        in_specs=[SMEM] * 4 + [VMEM] * 3,
        out_specs=(VMEM, VMEM),
        scratch_shapes=[
            pltpu.VMEM((tiles, width, 2 * width), F32),
            pltpu.VMEM((tiles, width, width), F32),
        ],
        compiler_params=pltpu.CompilerParams(vmem_limit_bytes=LIMIT),
        cost_estimate=pl.CostEstimate(
            flops=int(17e9), bytes_accessed=int(40e6), transcendentals=int(1e12)
        ),
        name="left_side",
    )(tile_rank, row_rank, target_rank, place, tile_u, near, far)


def right_side(band_rank, place, tile_v, near, far, panels, head):
    tiles, order, width = tile_v.shape
    return pl.pallas_call(
        right_kernel,
        out_shape=jax.ShapeDtypeStruct((1, tiles, order, width), BF16),
        in_specs=[SMEM] * 2 + [VMEM] * 5,
        out_specs=ANY,
        scratch_shapes=[
            pltpu.VMEM((tiles, order, width), BF16),
            pltpu.SemaphoreType.DMA((tiles,)),
        ],
        compiler_params=pltpu.CompilerParams(vmem_limit_bytes=LIMIT),
        cost_estimate=pl.CostEstimate(
            flops=int(2e9), bytes_accessed=int(10e6), transcendentals=0
        ),
        name="right_side",
    )(band_rank, place, tile_v, near, far, panels, head)


def copies_kernel(line, out, sems):
    stores = [pltpu.make_async_copy(line, out.at[k], sems.at[k]) for k in range(out.shape[0])]
    for store in stores:
        store.start()
    for store in stores:
        store.wait()


def copies_of(line, size):
    return pl.pallas_call(
        copies_kernel,
        out_shape=jax.ShapeDtypeStruct((size,) + line.shape, line.dtype),
        in_specs=[VMEM],
        out_specs=ANY,
        scratch_shapes=[pltpu.SemaphoreType.DMA((size,))],
        compiler_params=pltpu.CompilerParams(vmem_limit_bytes=LIMIT),
        name="copies",
    )(line)


def prepare_kernel(panel_u, panel_v, line, share, both, sems):
    loads = [
        pltpu.make_async_copy(x, share.at[k], sems.at[k]) for k, x in enumerate((panel_u, panel_v))
    ]
    for load in loads:
        load.start()
    for load in loads:
        load.wait()
    both[...] = share[...].astype(F32).reshape(both.shape).astype(BF16)
    stores = [pltpu.make_async_copy(both, line.at[k], sems.at[k]) for k in range(line.shape[0])]
    for store in stores:
        store.start()
    for store in stores:
        store.wait()


def prepare(panel_u, panel_v, size):
    tiles, share, width = panel_u.shape
    rows = 2 * tiles * share
    return pl.pallas_call(
        prepare_kernel,
        out_shape=jax.ShapeDtypeStruct((size, rows, width), BF16),
        in_specs=[ANY] * 2,
        out_specs=ANY,
        scratch_shapes=[
            pltpu.VMEM((2,) + panel_u.shape, BF16),
            pltpu.VMEM((rows, width), BF16),
            pltpu.SemaphoreType.DMA((size,)),
        ],
        compiler_params=pltpu.CompilerParams(vmem_limit_bytes=None),
        cost_estimate=pl.CostEstimate(
            flops=int(1e8), bytes_accessed=int(1e6), transcendentals=0
        ),
        name="prepare",
    )(panel_u, panel_v)


def join_kernel(row, across, near):
    near[0] = row[0]
    near[1] = across[0]


def join(row, across):
    return pl.pallas_call(
        join_kernel,
        out_shape=jax.ShapeDtypeStruct((2,) + row.shape[1:], row.dtype),
        in_specs=[VMEM] * 2,
        out_specs=VMEM,
        compiler_params=pltpu.CompilerParams(vmem_limit_bytes=LIMIT),
        name="join",
    )(row, across)


def swap(x, axis):
    return lax.ppermute(x, axis, [(0, 1), (1, 0)])


def on_device(
    tile_u, tile_v, tile_rank, panel_u, panel_v, band_rank, row_u, row_v, row_rank, target_rank
):
    tiles, share, width = panel_u.shape
    copies = prepare(panel_u, panel_v, 8)
    row = jnp.stack([row_u, row_v], axis=1)
    across = swap(row, "zh")
    line = lax.all_to_all(copies, "z", 0, 0, axis_index_groups=[ORDER], tiled=True)
    copies = copies_of(line, 16)
    panels = lax.all_to_all(copies, ("y", "x"), 0, 0, tiled=True)
    near = join(row, across)
    panels = lax.all_to_all(copies, ("y", "x"), 0, 0, tiled=True)
    far = swap(near, "core")
    place = jnp.stack([lax.axis_index("zh"), lax.axis_index("core")]).astype(jnp.int32)
    new_u, head = left_side(tile_rank, row_rank, target_rank, place, tile_u[0], near, far)
    panels = panels.reshape(128, 2 * tiles * share, width)
    new_v = right_side(band_rank, place, tile_v[0], near, far, panels, head)
    return new_u, new_v


def solution(mesh):
    fine = Mesh(mesh.devices.reshape(4, 4, 8, 2, 2), ("y", "x", "z", "zh", "core"))
    blk, col = ("y", "x", "z"), ("zh", "core")
    return jax.shard_map(
        on_device,
        mesh=fine,
        in_specs=(
            P(blk, col, None, None),
            P(blk, col, None, None),
            P(blk, col),
            P(col, blk, None),
            P(col, blk, None),
            P(col),
            P(blk, col, None),
            P(blk, col, None),
            P(blk),
            P(blk, col),
        ),
        out_specs=(P(blk, col, None, None), P(blk, col, None, None)),
        check_vma=False,
    )
```

```python
import math

import jax
import jax.numpy as jnp
from jax import lax
from jax.experimental import pallas as pl
from jax.experimental.pallas import tpu as pltpu
from jax.sharding import Mesh, PartitionSpec as P

F32, BF16 = jnp.float32, jnp.bfloat16
HIGH = lax.Precision.HIGHEST
STEP = 8
BLOCK = 16
ORDER = [3, 4, 2, 5, 1, 6, 0, 7]


def dot(a, b, dims, precision=None):
    return lax.dot_general(
        a, b, (dims, ((), ())), precision=precision, preferred_element_type=F32
    )


def three_parts(x):
    high = x.astype(BF16).astype(F32)
    rest = x - high
    middle = rest.astype(BF16).astype(F32)
    return high, middle, rest - middle


def spread(row):
    return jnp.broadcast_to(row, (BLOCK, row.shape[1]))


def factor_panel(panel, inverse, first):
    width = panel.shape[1]
    sub = lax.broadcasted_iota(jnp.int32, (BLOCK, width), 0)
    column = [
        jnp.broadcast_to(panel[:, first + s : first + s + 1], (BLOCK, width)) for s in range(BLOCK)
    ]
    for s in range(BLOCK - 1):
        ratio = jnp.where(sub > s, column[s] / spread(column[s][s : s + 1]), 0.0)
        panel = panel - ratio * spread(panel[s : s + 1])
        inverse = inverse - ratio * spread(inverse[s : s + 1])
        for u in range(s + 1, BLOCK):
            column[u] = column[u] - ratio * spread(column[u][s : s + 1])
    pivot = column[0]
    for s in range(1, BLOCK):
        pivot = jnp.where(sub == s, column[s], pivot)
    scale = lax.rsqrt(pivot)
    scale = scale * (1.5 - 0.5 * pivot * scale * scale)
    return panel * scale, inverse * scale


def left_kernel(
    tile_rank, row_rank, target_rank, place, tile_u, near, far, new_u, head, gram, lower_inv
):
    tiles, order, width = tile_u.shape
    quarter = order // 4
    lane = lax.broadcasted_iota(jnp.int32, (width, width), 1)
    sub = lax.broadcasted_iota(jnp.int32, (width, width), 0)
    rows = []
    for q in range(4):
        mine, other = place[0] ^ (q // 2), place[1] ^ (q % 2)
        rows.append(jnp.where(other == 0, near[mine, 0], far[mine, 0]))
    left_row = jnp.concatenate(rows, axis=0)
    pick_row = jnp.where((lane == 2 * sub + 1) & (sub < row_rank[0]), 1.0, 0.0)
    firsts, sides = [], []
    for t in range(tiles):
        pick_tile = jnp.where((lane == 2 * sub) & (sub < tile_rank[0, t]), 1.0, 0.0)
        pick = jnp.concatenate([pick_tile, pick_row], axis=0).astype(BF16)
        both = jnp.concatenate([tile_u[t], left_row], axis=1)
        first = dot(both, pick, ((1,), (0,))).astype(BF16)
        side = dot(first, jnp.concatenate([both, first], axis=1), ((0,), (0,)))
        half = sub // 2
        rank = jnp.where(sub % 2 == 0, tile_rank[0, t], row_rank[0])
        unit = jnp.where(lane == sub, 1.0, 0.0)
        gram[t, :, :width] = side[:, 2 * width :] + jnp.where(half >= rank, unit, 0.0)
        gram[t, :, width:] = unit
        firsts.append(first)
        tile_side = jnp.where(lane < tile_rank[0, t], side[:, :width], 0.0)
        row_side = jnp.where(lane < row_rank[0], side[:, width : 2 * width], 0.0)
        sides.append(jnp.concatenate([tile_side, row_side], axis=1))
    for first in range(0, width, BLOCK):
        later = first + BLOCK
        for t in range(tiles):
            upper, inverse = factor_panel(
                gram[t, first:later, :width], gram[t, first:later, width:], first
            )
            lower_inv[t, first:later, :] = inverse
            if later < width:
                uh, um, ul = three_parts(upper)
                ih, im, il = three_parts(inverse)
                a = jnp.concatenate([uh, uh, um, uh, um, ul], axis=0).astype(BF16)
                b = jnp.concatenate(
                    [
                        jnp.concatenate([uh, um, uh, ul, um, uh], axis=0),
                        jnp.concatenate([ih, im, ih, il, im, ih], axis=0),
                    ],
                    axis=1,
                ).astype(BF16)
                change = dot(a, b, ((0,), (0,)))
                gram[t, later:, :] = gram[t, later:, :] - change[later:, :]
    scale = math.sqrt(order)
    for t in range(tiles):
        solved = jnp.where(sub < target_rank[0, t], lower_inv[t], 0.0)
        head[t] = dot(solved, sides[t], ((1,), (0,)), HIGH) / scale
        solved = solved * scale
        high = solved.astype(BF16)
        low = (solved - high.astype(F32)).astype(BF16)
        new_u[0, t] = dot(
            jnp.concatenate([firsts[t], firsts[t]], axis=1),
            jnp.concatenate([high, low], axis=1),
            ((1,), (1,)),
        ).astype(BF16)


def right_kernel(band_rank, place, tile_v, near, far, panels, head, new_v, out_at, sems):
    tiles, order, width = tile_v.shape
    rows = []
    for q in range(4):
        mine, other = place[0] ^ (q // 2), place[1] ^ (q % 2)
        rows.append(jnp.where(other == 0, near[mine, 1], far[mine, 1]))
    right_row = jnp.concatenate(rows, axis=0)
    lane = lax.broadcasted_iota(jnp.int32, (width, width), 1)

    def panel_pair(which, pair):
        at = (which * tiles + pair) * STEP
        wide = panels[:, at : at + 2 * STEP, :].astype(F32)
        wide = wide.reshape(-1, len(ORDER), 2 * STEP, width)
        wide = jnp.stack([wide[:, ORDER.index(z)] for z in range(len(ORDER))], axis=1)
        return [
            wide[:, :, :STEP].reshape(order, width).astype(BF16),
            wide[:, :, STEP:].reshape(order, width).astype(BF16),
        ]

    panel_v = panel_pair(1, 0) + panel_pair(1, 2)
    core = dot(right_row, jnp.concatenate(panel_v, axis=1), ((0,), (0,)))
    weights = []
    for t in range(tiles):
        mixed = dot(head[t, :, width:], core[:, t * width : (t + 1) * width], ((1,), (0,)), HIGH)
        mixed = jnp.where(lane < band_rank[t], -mixed, 0.0)
        weight = jnp.concatenate([head[t, :, :width], mixed], axis=1)
        high = weight.astype(BF16)
        low = (weight - high.astype(F32)).astype(BF16)
        weights.append((high, low))
    stores = []
    for t in range(tiles):
        if t % 2 == 0:
            panel_u = panel_pair(0, t)
        high, low = weights[t]
        both = jnp.concatenate([tile_v[t], panel_u[t % 2]], axis=1)
        value = dot(both, jnp.concatenate([high, low], axis=0), ((1,), (1,)))
        out_at[t] = (value[:, :width] + value[:, width:]).astype(BF16)
        stores.append(pltpu.make_async_copy(out_at.at[t], new_v.at[0, t], sems.at[t]))
        stores[t].start()
    for store in stores:
        store.wait()


SMEM = pl.BlockSpec(memory_space=pltpu.SMEM)
VMEM = pl.BlockSpec(memory_space=pltpu.VMEM)
ANY = pl.BlockSpec(memory_space=pl.ANY)
LIMIT = 16 * 1024 * 1024


def left_side(tile_rank, row_rank, target_rank, place, tile_u, near, far):
    tiles, order, width = tile_u.shape
    return pl.pallas_call(
        left_kernel,
        out_shape=(
            jax.ShapeDtypeStruct((1, tiles, order, width), BF16),
            jax.ShapeDtypeStruct((tiles, width, 2 * width), F32),
        ),
        in_specs=[SMEM] * 4 + [VMEM] * 3,
        out_specs=(VMEM, VMEM),
        scratch_shapes=[
            pltpu.VMEM((tiles, width, 2 * width), F32),
            pltpu.VMEM((tiles, width, width), F32),
        ],
        compiler_params=pltpu.CompilerParams(vmem_limit_bytes=LIMIT),
        cost_estimate=pl.CostEstimate(
            flops=int(17e9), bytes_accessed=int(40e6), transcendentals=int(1e12)
        ),
        name="left_side",
    )(tile_rank, row_rank, target_rank, place, tile_u, near, far)


def right_side(band_rank, place, tile_v, near, far, panels, head):
    tiles, order, width = tile_v.shape
    return pl.pallas_call(
        right_kernel,
        out_shape=jax.ShapeDtypeStruct((1, tiles, order, width), BF16),
        in_specs=[SMEM] * 2 + [VMEM] * 5,
        out_specs=ANY,
        scratch_shapes=[
            pltpu.VMEM((tiles, order, width), BF16),
            pltpu.SemaphoreType.DMA((tiles,)),
        ],
        compiler_params=pltpu.CompilerParams(vmem_limit_bytes=LIMIT),
        cost_estimate=pl.CostEstimate(
            flops=int(2e9), bytes_accessed=int(10e6), transcendentals=0
        ),
        name="right_side",
    )(band_rank, place, tile_v, near, far, panels, head)


def copies_kernel(line, out, sems):
    stores = [pltpu.make_async_copy(line, out.at[k], sems.at[k]) for k in range(out.shape[0])]
    for store in stores:
        store.start()
    for store in stores:
        store.wait()


def copies_of(line, size):
    return pl.pallas_call(
        copies_kernel,
        out_shape=jax.ShapeDtypeStruct((size,) + line.shape, line.dtype),
        in_specs=[VMEM],
        out_specs=ANY,
        scratch_shapes=[pltpu.SemaphoreType.DMA((size,))],
        compiler_params=pltpu.CompilerParams(vmem_limit_bytes=LIMIT),
        name="copies",
    )(line)


def prepare_kernel(panel_u, panel_v, row_u, row_v, line, row, share, both, rows, sems):
    sources = (panel_u, panel_v, row_u, row_v)
    targets = (share.at[0], share.at[1], rows.at[:, 0], rows.at[:, 1])
    loads = [pltpu.make_async_copy(sources[k], targets[k], sems.at[k]) for k in range(4)]
    for load in loads:
        load.start()
    for load in loads[:2]:
        load.wait()
    both[...] = share[...].astype(F32).reshape(both.shape).astype(BF16)
    stores = [
        pltpu.make_async_copy(both, line.at[k], sems.at[5 + k]) for k in range(line.shape[0])
    ]
    for store in stores:
        store.start()
    for load in loads[2:]:
        load.wait()
    stores.append(pltpu.make_async_copy(rows, row, sems.at[4]))
    stores[-1].start()
    for store in stores:
        store.wait()


def prepare(panel_u, panel_v, row_u, row_v, size):
    tiles, share, width = panel_u.shape
    rows = 2 * tiles * share
    return pl.pallas_call(
        prepare_kernel,
        out_shape=(
            jax.ShapeDtypeStruct((size, rows, width), BF16),
            jax.ShapeDtypeStruct((1, 2) + row_u.shape[1:], BF16),
        ),
        in_specs=[ANY] * 4,
        out_specs=(ANY, ANY),
        scratch_shapes=[
            pltpu.VMEM((2,) + panel_u.shape, BF16),
            pltpu.VMEM((rows, width), BF16),
            pltpu.VMEM((1, 2) + row_u.shape[1:], BF16),
            pltpu.SemaphoreType.DMA((5 + size,)),
        ],
        compiler_params=pltpu.CompilerParams(vmem_limit_bytes=None),
        cost_estimate=pl.CostEstimate(
            flops=int(1e8), bytes_accessed=int(1e6), transcendentals=0
        ),
        name="prepare",
    )(panel_u, panel_v, row_u, row_v)


def join_kernel(row, across, near):
    near[0] = row[0]
    near[1] = across[0]


def join(row, across):
    return pl.pallas_call(
        join_kernel,
        out_shape=jax.ShapeDtypeStruct((2,) + row.shape[1:], row.dtype),
        in_specs=[VMEM] * 2,
        out_specs=VMEM,
        compiler_params=pltpu.CompilerParams(vmem_limit_bytes=LIMIT),
        name="join",
    )(row, across)


def swap(x, axis):
    return lax.ppermute(x, axis, [(0, 1), (1, 0)])


def on_device(
    tile_u, tile_v, tile_rank, panel_u, panel_v, band_rank, row_u, row_v, row_rank, target_rank
):
    tiles, share, width = panel_u.shape
    copies, row = prepare(panel_u, panel_v, row_u, row_v, 8)
    across = swap(row, "zh")
    line = lax.all_to_all(copies, "z", 0, 0, axis_index_groups=[ORDER], tiled=True)
    copies = copies_of(line, 16)
    panels = lax.all_to_all(copies, ("y", "x"), 0, 0, tiled=True)
    near = join(row, across)
    panels = lax.all_to_all(copies, ("y", "x"), 0, 0, tiled=True)
    far = swap(near, "core")
    place = jnp.stack([lax.axis_index("zh"), lax.axis_index("core")]).astype(jnp.int32)
    new_u, head = left_side(tile_rank, row_rank, target_rank, place, tile_u[0], near, far)
    panels = panels.reshape(128, 2 * tiles * share, width)
    new_v = right_side(band_rank, place, tile_v[0], near, far, panels, head)
    return new_u, new_v


def solution(mesh):
    fine = Mesh(mesh.devices.reshape(4, 4, 8, 2, 2), ("y", "x", "z", "zh", "core"))
    blk, col = ("y", "x", "z"), ("zh", "core")
    return jax.shard_map(
        on_device,
        mesh=fine,
        in_specs=(
            P(blk, col, None, None),
            P(blk, col, None, None),
            P(blk, col),
            P(col, blk, None),
            P(col, blk, None),
            P(col),
            P(blk, col, None),
            P(blk, col, None),
            P(blk),
            P(blk, col),
        ),
        out_specs=(P(blk, col, None, None), P(blk, col, None, None)),
        check_vma=False,
    )
```

```python
import math

import jax
import jax.numpy as jnp
from jax import lax
from jax.experimental import pallas as pl
from jax.experimental.pallas import tpu as pltpu
from jax.sharding import Mesh, PartitionSpec as P

F32, BF16 = jnp.float32, jnp.bfloat16
HIGH = lax.Precision.HIGHEST
STEP = 8
BLOCK = 16
ORDER = [3, 4, 2, 5, 1, 6, 0, 7]
PLANE = [0, 1, 3, 2, 4, 5, 7, 6, 12, 13, 15, 14, 8, 9, 11, 10]


def dot(a, b, dims, precision=None):
    return lax.dot_general(
        a, b, (dims, ((), ())), precision=precision, preferred_element_type=F32
    )


def three_parts(x):
    high = x.astype(BF16).astype(F32)
    rest = x - high
    middle = rest.astype(BF16).astype(F32)
    return high, middle, rest - middle


def spread(row):
    return jnp.broadcast_to(row, (BLOCK, row.shape[1]))


def factor_panel(panel, inverse, first):
    width = panel.shape[1]
    sub = lax.broadcasted_iota(jnp.int32, (BLOCK, width), 0)
    column = [
        jnp.broadcast_to(panel[:, first + s : first + s + 1], (BLOCK, width)) for s in range(BLOCK)
    ]
    for s in range(BLOCK - 1):
        ratio = jnp.where(sub > s, column[s] / spread(column[s][s : s + 1]), 0.0)
        panel = panel - ratio * spread(panel[s : s + 1])
        inverse = inverse - ratio * spread(inverse[s : s + 1])
        for u in range(s + 1, BLOCK):
            column[u] = column[u] - ratio * spread(column[u][s : s + 1])
    pivot = column[0]
    for s in range(1, BLOCK):
        pivot = jnp.where(sub == s, column[s], pivot)
    scale = lax.rsqrt(pivot)
    scale = scale * (1.5 - 0.5 * pivot * scale * scale)
    return panel * scale, inverse * scale


def left_kernel(
    tile_rank, row_rank, target_rank, place, tile_u, near, far, new_u, head, gram, lower_inv
):
    tiles, order, width = tile_u.shape
    quarter = order // 4
    lane = lax.broadcasted_iota(jnp.int32, (width, width), 1)
    sub = lax.broadcasted_iota(jnp.int32, (width, width), 0)
    rows = []
    for q in range(4):
        mine, other = place[0] ^ (q // 2), place[1] ^ (q % 2)
        rows.append(jnp.where(other == 0, near[mine, 0], far[mine, 0]))
    left_row = jnp.concatenate(rows, axis=0)
    pick_row = jnp.where((lane == 2 * sub + 1) & (sub < row_rank[0]), 1.0, 0.0)
    firsts, sides = [], []
    for t in range(tiles):
        pick_tile = jnp.where((lane == 2 * sub) & (sub < tile_rank[0, t]), 1.0, 0.0)
        pick = jnp.concatenate([pick_tile, pick_row], axis=0).astype(BF16)
        both = jnp.concatenate([tile_u[t], left_row], axis=1)
        first = dot(both, pick, ((1,), (0,))).astype(BF16)
        side = dot(first, jnp.concatenate([both, first], axis=1), ((0,), (0,)))
        half = sub // 2
        rank = jnp.where(sub % 2 == 0, tile_rank[0, t], row_rank[0])
        unit = jnp.where(lane == sub, 1.0, 0.0)
        gram[t, :, :width] = side[:, 2 * width :] + jnp.where(half >= rank, unit, 0.0)
        gram[t, :, width:] = unit
        firsts.append(first)
        tile_side = jnp.where(lane < tile_rank[0, t], side[:, :width], 0.0)
        row_side = jnp.where(lane < row_rank[0], side[:, width : 2 * width], 0.0)
        sides.append(jnp.concatenate([tile_side, row_side], axis=1))
    for first in range(0, width, BLOCK):
        later = first + BLOCK
        for t in range(tiles):
            upper, inverse = factor_panel(
                gram[t, first:later, :width], gram[t, first:later, width:], first
            )
            lower_inv[t, first:later, :] = inverse
            if later < width:
                uh, um, ul = three_parts(upper)
                ih, im, il = three_parts(inverse)
                a = jnp.concatenate([uh, uh, um, uh, um, ul], axis=0).astype(BF16)
                b = jnp.concatenate(
                    [
                        jnp.concatenate([uh, um, uh, ul, um, uh], axis=0),
                        jnp.concatenate([ih, im, ih, il, im, ih], axis=0),
                    ],
                    axis=1,
                ).astype(BF16)
                change = dot(a, b, ((0,), (0,)))
                gram[t, later:, :] = gram[t, later:, :] - change[later:, :]
    scale = math.sqrt(order)
    for t in range(tiles):
        solved = jnp.where(sub < target_rank[0, t], lower_inv[t], 0.0)
        head[t] = dot(solved, sides[t], ((1,), (0,)), HIGH) / scale
        solved = solved * scale
        high = solved.astype(BF16)
        low = (solved - high.astype(F32)).astype(BF16)
        new_u[0, t] = dot(
            jnp.concatenate([firsts[t], firsts[t]], axis=1),
            jnp.concatenate([high, low], axis=1),
            ((1,), (1,)),
        ).astype(BF16)


def right_kernel(band_rank, place, tile_v, near, far, panels, head, new_v, out_at, sems):
    tiles, order, width = tile_v.shape
    rows = []
    for q in range(4):
        mine, other = place[0] ^ (q // 2), place[1] ^ (q % 2)
        rows.append(jnp.where(other == 0, near[mine, 1], far[mine, 1]))
    right_row = jnp.concatenate(rows, axis=0)
    lane = lax.broadcasted_iota(jnp.int32, (width, width), 1)

    def panel_pair(which, pair):
        at = (which * tiles + pair) * STEP
        wide = panels[:, at : at + 2 * STEP, :].astype(F32)
        places = [
            PLANE.index(p) * len(ORDER) + ORDER.index(z)
            for p in range(len(PLANE))
            for z in range(len(ORDER))
        ]
        wide = jnp.stack([wide[k] for k in places])
        return [
            wide[:, :STEP].reshape(order, width).astype(BF16),
            wide[:, STEP:].reshape(order, width).astype(BF16),
        ]

    panel_v = panel_pair(1, 0) + panel_pair(1, 2)
    core = dot(right_row, jnp.concatenate(panel_v, axis=1), ((0,), (0,)))
    weights = []
    for t in range(tiles):
        mixed = dot(head[t, :, width:], core[:, t * width : (t + 1) * width], ((1,), (0,)), HIGH)
        mixed = jnp.where(lane < band_rank[t], -mixed, 0.0)
        weight = jnp.concatenate([head[t, :, :width], mixed], axis=1)
        high = weight.astype(BF16)
        low = (weight - high.astype(F32)).astype(BF16)
        weights.append((high, low))
    stores = []
    for t in range(tiles):
        if t % 2 == 0:
            panel_u = panel_pair(0, t)
        high, low = weights[t]
        both = jnp.concatenate([tile_v[t], panel_u[t % 2]], axis=1)
        value = dot(both, jnp.concatenate([high, low], axis=0), ((1,), (1,)))
        out_at[t] = (value[:, :width] + value[:, width:]).astype(BF16)
        stores.append(pltpu.make_async_copy(out_at.at[t], new_v.at[0, t], sems.at[t]))
        stores[t].start()
    for store in stores:
        store.wait()


SMEM = pl.BlockSpec(memory_space=pltpu.SMEM)
VMEM = pl.BlockSpec(memory_space=pltpu.VMEM)
ANY = pl.BlockSpec(memory_space=pl.ANY)
LIMIT = 16 * 1024 * 1024


def left_side(tile_rank, row_rank, target_rank, place, tile_u, near, far):
    tiles, order, width = tile_u.shape
    return pl.pallas_call(
        left_kernel,
        out_shape=(
            jax.ShapeDtypeStruct((1, tiles, order, width), BF16),
            jax.ShapeDtypeStruct((tiles, width, 2 * width), F32),
        ),
        in_specs=[SMEM] * 4 + [VMEM] * 3,
        out_specs=(VMEM, VMEM),
        scratch_shapes=[
            pltpu.VMEM((tiles, width, 2 * width), F32),
            pltpu.VMEM((tiles, width, width), F32),
        ],
        compiler_params=pltpu.CompilerParams(vmem_limit_bytes=LIMIT),
        cost_estimate=pl.CostEstimate(
            flops=int(17e9), bytes_accessed=int(40e6), transcendentals=int(1e12)
        ),
        name="left_side",
    )(tile_rank, row_rank, target_rank, place, tile_u, near, far)


def right_side(band_rank, place, tile_v, near, far, panels, head):
    tiles, order, width = tile_v.shape
    return pl.pallas_call(
        right_kernel,
        out_shape=jax.ShapeDtypeStruct((1, tiles, order, width), BF16),
        in_specs=[SMEM] * 2 + [VMEM] * 5,
        out_specs=ANY,
        scratch_shapes=[
            pltpu.VMEM((tiles, order, width), BF16),
            pltpu.SemaphoreType.DMA((tiles,)),
        ],
        compiler_params=pltpu.CompilerParams(vmem_limit_bytes=LIMIT),
        cost_estimate=pl.CostEstimate(
            flops=int(2e9), bytes_accessed=int(10e6), transcendentals=0
        ),
        name="right_side",
    )(band_rank, place, tile_v, near, far, panels, head)


def copies_kernel(line, out, sems):
    stores = [pltpu.make_async_copy(line, out.at[k], sems.at[k]) for k in range(out.shape[0])]
    for store in stores:
        store.start()
    for store in stores:
        store.wait()


def copies_of(line, size):
    return pl.pallas_call(
        copies_kernel,
        out_shape=jax.ShapeDtypeStruct((size,) + line.shape, line.dtype),
        in_specs=[VMEM],
        out_specs=ANY,
        scratch_shapes=[pltpu.SemaphoreType.DMA((size,))],
        compiler_params=pltpu.CompilerParams(vmem_limit_bytes=LIMIT),
        name="copies",
    )(line)


def prepare_kernel(panel_u, panel_v, row_u, row_v, line, row, share, both, rows, sems):
    sources = (panel_u, panel_v, row_u, row_v)
    targets = (share.at[0], share.at[1], rows.at[:, 0], rows.at[:, 1])
    loads = [pltpu.make_async_copy(sources[k], targets[k], sems.at[k]) for k in range(4)]
    for load in loads:
        load.start()
    for load in loads[:2]:
        load.wait()
    both[...] = share[...].astype(F32).reshape(both.shape).astype(BF16)
    stores = [
        pltpu.make_async_copy(both, line.at[k], sems.at[5 + k]) for k in range(line.shape[0])
    ]
    for store in stores:
        store.start()
    for load in loads[2:]:
        load.wait()
    stores.append(pltpu.make_async_copy(rows, row, sems.at[4]))
    stores[-1].start()
    for store in stores:
        store.wait()


def prepare(panel_u, panel_v, row_u, row_v, size):
    tiles, share, width = panel_u.shape
    rows = 2 * tiles * share
    return pl.pallas_call(
        prepare_kernel,
        out_shape=(
            jax.ShapeDtypeStruct((size, rows, width), BF16),
            jax.ShapeDtypeStruct((1, 2) + row_u.shape[1:], BF16),
        ),
        in_specs=[ANY] * 4,
        out_specs=(ANY, ANY),
        scratch_shapes=[
            pltpu.VMEM((2,) + panel_u.shape, BF16),
            pltpu.VMEM((rows, width), BF16),
            pltpu.VMEM((1, 2) + row_u.shape[1:], BF16),
            pltpu.SemaphoreType.DMA((5 + size,)),
        ],
        compiler_params=pltpu.CompilerParams(vmem_limit_bytes=None),
        cost_estimate=pl.CostEstimate(
            flops=int(1e8), bytes_accessed=int(1e6), transcendentals=0
        ),
        name="prepare",
    )(panel_u, panel_v, row_u, row_v)


def join_kernel(row, across, near):
    near[0] = row[0]
    near[1] = across[0]


def join(row, across):
    return pl.pallas_call(
        join_kernel,
        out_shape=jax.ShapeDtypeStruct((2,) + row.shape[1:], row.dtype),
        in_specs=[VMEM] * 2,
        out_specs=VMEM,
        compiler_params=pltpu.CompilerParams(vmem_limit_bytes=LIMIT),
        name="join",
    )(row, across)


def swap(x, axis):
    return lax.ppermute(x, axis, [(0, 1), (1, 0)])


def on_device(
    tile_u, tile_v, tile_rank, panel_u, panel_v, band_rank, row_u, row_v, row_rank, target_rank
):
    tiles, share, width = panel_u.shape
    copies, row = prepare(panel_u, panel_v, row_u, row_v, 8)
    across = swap(row, "zh")
    line = lax.all_to_all(copies, "z", 0, 0, axis_index_groups=[ORDER], tiled=True)
    copies = copies_of(line, 16)
    panels = lax.all_to_all(
        copies, ("y", "x"), 0, 0, axis_index_groups=[PLANE], tiled=True
    )
    near = join(row, across)
    panels = lax.all_to_all(
        copies, ("y", "x"), 0, 0, axis_index_groups=[PLANE], tiled=True
    )
    far = swap(near, "core")
    place = jnp.stack([lax.axis_index("zh"), lax.axis_index("core")]).astype(jnp.int32)
    new_u, head = left_side(tile_rank, row_rank, target_rank, place, tile_u[0], near, far)
    panels = panels.reshape(128, 2 * tiles * share, width)
    new_v = right_side(band_rank, place, tile_v[0], near, far, panels, head)
    return new_u, new_v


def solution(mesh):
    fine = Mesh(mesh.devices.reshape(4, 4, 8, 2, 2), ("y", "x", "z", "zh", "core"))
    blk, col = ("y", "x", "z"), ("zh", "core")
    return jax.shard_map(
        on_device,
        mesh=fine,
        in_specs=(
            P(blk, col, None, None),
            P(blk, col, None, None),
            P(blk, col),
            P(col, blk, None),
            P(col, blk, None),
            P(col),
            P(blk, col, None),
            P(blk, col, None),
            P(blk),
            P(blk, col),
        ),
        out_specs=(P(blk, col, None, None), P(blk, col, None, None)),
        check_vma=False,
    )
```
